256 devices in a mesh: grp: 8 (over y, core), sp: 32 (over z, x).
Axes of the slice: x: 4, y: 4, z: 8, core: 2. Of those that a mesh axis runs over, the one named last changes fastest.
Arguments:
- query: bfloat16 [32768, 4096], P(('grp', 'sp')), parts along dimension 0, may hold values from -24 to 24
- keys: bfloat16 [32768, 512], P(('grp', 'sp')), parts along dimension 0, may hold values from -4 to 4
- values: bfloat16 [32768, 512], P(('grp', 'sp')), parts along dimension 0, may hold values from -6 to 6
- out_grad: bfloat16 [32768, 4096], P(('grp', 'sp')), parts along dimension 0, may hold values from -6 to 6
- documents: int32 [32768], P(('grp', 'sp')), parts along dimension 0, may hold values from 0 to 7, never falling along the last dimension, each value on 1 to 2048 neighbouring positions
Outputs:
- attn_out: bfloat16 [32768, 4096], P(('grp', 'sp')), parts along dimension 0
- query_grad: bfloat16 [32768, 4096], P(('grp', 'sp')), parts along dimension 0
- key_grad: bfloat16 [32768, 512], P(('grp', 'sp')), parts along dimension 0
- value_grad: bfloat16 [32768, 512], P(('grp', 'sp')), parts along dimension 0
The draws below stay inside these ranges and needn't reach their ends.
There are 8 independent parts, one for each index of `grp`. The reference program is written for one: setup_inputs(seed, part) draws one part's arguments, and reference() takes and returns one part's arrays. A program takes and returns all parts, laid end to end along the dimension named above; each array names one. Nothing has to cross between parts.
Inputs may be any that keep to these rules, and one draw needn't show every extreme that they name: `documents`: document ids never fall along the window; each document holds 1 to 2048 tokens and one holds exactly 2048.
All inputs are finite; a program needn't handle non-finite values.
Results may differ from the reference program's by a relative error of at most 0.019.
Values may be sent and summed in bfloat16 or wider, within the bound.
A program may use at most 128 MiB of HBM per device.

```python
import math
import jax
import jax.numpy as jnp
import numpy as np
from jax import lax

QH = 32
KVH = 4
HD = 128
DOCS = 8
TOKENS = 4096
GROUP = 8
MOST_DOC = 2048


def draw_keys(key, part):
    key = jax.random.fold_in(key, 7)
    return jax.random.truncated_normal(key, -4.0, 4.0, (TOKENS, KVH * HD), jnp.float32).astype(jnp.bfloat16)


def draw_query(key, part):
    key = jax.random.fold_in(key, 9)
    return jax.random.truncated_normal(key, -4.0, 4.0, (TOKENS, QH * HD), jnp.float32).astype(jnp.bfloat16)


def block_scale(rng, shape, cuts, smallest, high):
    level, own = 1.0, jax.random.fold_in(rng, 6)
    for axis_at, shards_of in cuts:
        heights = jnp.exp(jax.random.uniform(jax.random.fold_in(own, axis_at), (shards_of,), jnp.float32, smallest / len(cuts), high / len(cuts)))
        level = level * jnp.repeat(heights, shape[axis_at] // shards_of).reshape([-1 if axis == axis_at else 1 for axis in range(len(shape))])
    return level


def profile(amount, total, bound, lean):
    weights = [(1 << 20) // math.isqrt(grade ** lean) + 1 for grade in range(2, amount + 1)]
    rest, holding = total - bound - (amount - 1), [1] * (amount - 1)
    while rest > 0:
        candidates = [i for i in range(amount - 1) if holding[i] < bound]
        mass, remaining = sum([weights[i] for i in candidates]), rest
        for i in candidates:
            more = min(bound - holding[i], max(1, remaining * weights[i] // mass), rest)
            holding[i] = holding[i] + more
            rest = rest - more
    return np.array([bound] + holding)


def uneven_parts(rng, count, total, bound, lean):
    if count == 2:
        one = jax.random.randint(rng, (), max(1, total - bound), min(bound, total - 1) + 1)
        return jnp.stack([one, total - one])
    tallies = jnp.asarray(profile(count, total, bound, lean), jnp.int32)
    twos = (count - 1) // 2
    donor, receiver = tallies[1:1 + 2 * twos:2], tallies[2:2 + 2 * twos:2]
    slack = jnp.minimum(donor - 1, bound - receiver)
    passed = jax.random.randint(jax.random.fold_in(rng, 1), (twos,), 0, 1 << 20) % (slack + 1)
    tallies = tallies.at[1:1 + 2 * twos:2].set(donor - passed).at[2:2 + 2 * twos:2].set(receiver + passed)
    return tallies[jax.random.permutation(jax.random.fold_in(rng, 2), count)]


def scatter_about(key, shape, deviation, reach, split=(), kind=jnp.bfloat16):
    gain = block_scale(key, shape, split, -0.22, 0.18) if split else 1.0
    drawn = jax.random.normal(key, shape, jnp.float32) * deviation * gain
    return jnp.minimum(jnp.maximum(drawn, -reach), reach).astype(kind)


def setup_inputs(seed: int = 0, part: int = 0) -> dict:
    arg_keys = jax.random.split(jax.random.key(seed), 6)
    own_keys = jax.random.split(jax.random.fold_in(arg_keys[5], part), 6)
    return {
        "query": draw_query(jax.random.fold_in(jax.random.fold_in(arg_keys[5], part), 71), part),
        "keys": draw_keys(jax.random.fold_in(jax.random.fold_in(arg_keys[5], part), 71), part),
        "values": scatter_about(own_keys[2], (TOKENS, KVH * HD), 1.0, 6.0, ((0, 32),)),
        "out_grad": scatter_about(own_keys[3], (TOKENS, QH * HD), 1.0, 6.0, ((0, 32),)),
        "documents": jnp.searchsorted(jnp.cumsum(uneven_parts(own_keys[4], DOCS, TOKENS, MOST_DOC, 1)), jnp.arange(TOKENS), side="right").astype(jnp.int32),
    }


very_low = -1e+30

def narrow(array):
    return lax.optimization_barrier(array.astype(jnp.bfloat16)).astype(jnp.float32)

def unchanged(state_in):
    return state_in

def tile_attention(query, keys, values, out_grad, row_docs_all, col_docs_all, row_offset):
    row_count, head_count, head_width = query.shape
    col_count, kv_heads = (keys.shape[0], keys.shape[1])
    group_size = head_count // kv_heads
    scale_factor = 1.0 / math.sqrt(head_width)
    row_block = math.gcd(row_count, 512)
    col_block = math.gcd(col_count, 512)
    col_steps = col_count // col_block
    query_split = query.reshape(row_count, kv_heads, group_size, head_width)
    grad_split = out_grad.reshape(row_count, kv_heads, group_size, head_width)
    col_positions = jnp.arange(col_count, dtype=jnp.int32)
    stat_shape = (kv_heads, group_size, row_block)

    def row_step(row_index, state_in):
        out_all, dq_all, dk_all, dv_all = state_in
        first_row = row_index * row_block
        q_blk = lax.dynamic_slice_in_dim(query_split, first_row, row_block, 0)
        g_blk = lax.dynamic_slice_in_dim(grad_split, first_row, row_block, 0)
        row_docs = lax.dynamic_slice_in_dim(row_docs_all, first_row, row_block, 0)
        row_pos = row_offset + first_row + jnp.arange(row_block, dtype=jnp.int32)

        def touched(col_index):
            col_start = col_index * col_block
            col_docs = lax.dynamic_slice_in_dim(col_docs_all, col_start, col_block, 0)
            return (col_start <= row_pos[-1]) & (col_docs[0] <= row_docs[-1]) & (row_docs[0] <= col_docs[-1])

        def tile_inputs(col_index):
            col_start = col_index * col_block
            k_blk = lax.dynamic_slice_in_dim(keys, col_start, col_block, 0)
            v_blk = lax.dynamic_slice_in_dim(values, col_start, col_block, 0)
            col_docs = lax.dynamic_slice_in_dim(col_docs_all, col_start, col_block, 0)
            col_pos = lax.dynamic_slice_in_dim(col_positions, col_start, col_block, 0)
            allowed = (row_docs[:, None] == col_docs[None, :]) & (col_pos[None, :] <= row_pos[:, None])
            scores = jnp.einsum('rkgd,ckd->kgrc', q_blk, k_blk, preferred_element_type=jnp.float32) * scale_factor
            return (col_start, k_blk, v_blk, allowed, scores)

        def stats_step(col_index, state_stat):

            def update(stat_pair):
                row_max, row_total = stat_pair
                _, _, _, allowed, scores = tile_inputs(col_index)
                tile_max = lax.optimization_barrier(jnp.max(jnp.where(allowed, scores, very_low), axis=-1))
                new_max = jnp.maximum(row_max, tile_max)
                shares = jnp.where(allowed, jnp.exp(scores - new_max[..., None]), 0.0)
                return (new_max, row_total * jnp.exp(row_max - new_max) + lax.optimization_barrier(jnp.sum(shares, axis=-1)))
            return lax.cond(touched(col_index), update, unchanged, state_stat)
        row_max, row_total = lax.fori_loop(0, col_steps, stats_step, (jnp.full(stat_shape, very_low, jnp.float32), jnp.zeros(stat_shape, jnp.float32)))
        log_total = row_max + jnp.log(row_total)

        def out_step(col_index, out_acc):

            def update(acc_in):
                _, _, v_blk, allowed, scores = tile_inputs(col_index)
                weights = narrow(jnp.where(allowed, jnp.exp(scores - log_total[..., None]), 0.0))
                return acc_in + jnp.einsum('kgrc,ckd->kgrd', weights, v_blk, preferred_element_type=jnp.float32)
            return lax.cond(touched(col_index), update, unchanged, out_acc)
        out_acc = lax.fori_loop(0, col_steps, out_step, jnp.zeros(stat_shape + (head_width,), jnp.float32))
        out_blk = narrow(jnp.transpose(out_acc, (2, 0, 1, 3)))
        row_delta = jnp.transpose(lax.optimization_barrier(jnp.sum(g_blk * out_blk, axis=-1)), (1, 2, 0))

        def grad_step(col_index, grad_state):

            def update(state_grad):
                dq_acc, dk_acc, dv_acc = state_grad
                col_start, k_blk, v_blk, allowed, scores = tile_inputs(col_index)
                weights = jnp.where(allowed, jnp.exp(scores - log_total[..., None]), 0.0)
                pushed = jnp.einsum('rkgd,ckd->kgrc', g_blk, v_blk, preferred_element_type=jnp.float32)
                slopes = narrow(weights * (pushed - row_delta[..., None]))
                dq_acc = dq_acc + jnp.einsum('kgrc,ckd->kgrd', slopes, k_blk, preferred_element_type=jnp.float32)
                dk_tile = jnp.einsum('kgrc,rkgd->ckd', slopes, q_blk, preferred_element_type=jnp.float32)
                dv_tile = jnp.einsum('kgrc,rkgd->ckd', narrow(weights), g_blk, preferred_element_type=jnp.float32)
                dk_acc = lax.dynamic_update_slice_in_dim(dk_acc, lax.dynamic_slice_in_dim(dk_acc, col_start, col_block, 0) + dk_tile, col_start, 0)
                dv_acc = lax.dynamic_update_slice_in_dim(dv_acc, lax.dynamic_slice_in_dim(dv_acc, col_start, col_block, 0) + dv_tile, col_start, 0)
                return (dq_acc, dk_acc, dv_acc)
            return lax.cond(touched(col_index), update, unchanged, grad_state)
        dq_acc, dk_all, dv_all = lax.fori_loop(0, col_steps, grad_step, (jnp.zeros(stat_shape + (head_width,), jnp.float32), dk_all, dv_all))
        out_all = lax.dynamic_update_slice_in_dim(out_all, out_blk, first_row, 0)
        dq_all = lax.dynamic_update_slice_in_dim(dq_all, jnp.transpose(dq_acc, (2, 0, 1, 3)), first_row, 0)
        return (out_all, dq_all, dk_all, dv_all)
    initial = (jnp.zeros((row_count, kv_heads, group_size, head_width), jnp.float32), jnp.zeros((row_count, kv_heads, group_size, head_width), jnp.float32), jnp.zeros((col_count, kv_heads, head_width), jnp.float32), jnp.zeros((col_count, kv_heads, head_width), jnp.float32))
    out_all, dq_all, dk_all, dv_all = lax.fori_loop(0, row_count // row_block, row_step, initial)
    return (out_all.reshape(row_count, head_count * head_width), (dq_all * scale_factor).reshape(row_count, head_count * head_width), dk_all * scale_factor, dv_all)

def reference(query, keys, values, out_grad, documents):
    query_heads = jnp.transpose(query.astype(jnp.float32).reshape(TOKENS, KVH, GROUP, HD), (1, 0, 2, 3))
    key_heads = jnp.transpose(keys.astype(jnp.float32).reshape(TOKENS, KVH, 1, HD), (1, 0, 2, 3))
    value_heads = jnp.transpose(values.astype(jnp.float32).reshape(TOKENS, KVH, 1, HD), (1, 0, 2, 3))
    grad_heads = jnp.transpose(out_grad.astype(jnp.float32).reshape(TOKENS, KVH, GROUP, HD), (1, 0, 2, 3))

    def one_group(head_items):
        q_part, k_part, v_part, g_part = head_items
        return tile_attention(q_part, k_part, v_part, g_part, documents, documents, 0)
    out_all, dq_all, dk_all, dv_all = lax.map(one_group, (query_heads, key_heads, value_heads, grad_heads))
    attn_out = jnp.transpose(out_all, (1, 0, 2)).reshape(TOKENS, QH * HD).astype(jnp.bfloat16)
    query_grad = jnp.transpose(dq_all, (1, 0, 2)).reshape(TOKENS, QH * HD).astype(jnp.bfloat16)
    key_grad = jnp.transpose(dk_all[:, :, 0, :], (1, 0, 2)).reshape(TOKENS, KVH * HD).astype(jnp.bfloat16)
    value_grad = jnp.transpose(dv_all[:, :, 0, :], (1, 0, 2)).reshape(TOKENS, KVH * HD).astype(jnp.bfloat16)
    return (attn_out, query_grad, key_grad, value_grad)
```

```python
import math

import jax
import jax.numpy as jnp
from jax import lax
from jax.experimental import pallas as pl
from jax.experimental.pallas import tpu as pltpu
from jax.sharding import PartitionSpec as P

HD = 128
TOK = 128
NX = 4
NZ = 8
GROUP = 8
ROWS = NX * TOK
HALF = ROWS // 2
FAR = 4
WIDE = GROUP * HD
UNROLL = 2
BIG = float(2**20)
LOW = -1e30
SCALE = 1.0 / math.sqrt(HD)
LOG2E = math.log2(math.e)
MESH = pl.DeviceIdType.MESH
F32, BF16 = jnp.float32, jnp.bfloat16

I_K, I_V, I_DOC, I_Q0, I_Q1, I_G, I_O, I_DQ0, I_DQ1, I_DK, I_DV = range(11)


def dot_nt(a, b):
    return lax.dot_general(a, b, (((1,), (1,)), ((), ())), preferred_element_type=F32)


def dot_nn(a, b):
    return lax.dot_general(a, b, (((1,), (0,)), ((), ())), preferred_element_type=F32)


def rows_of(far, half):
    if far == 0 and half == 1:
        return HALF, HALF
    if far == FAR and half == 0:
        return 0, HALF
    return 0, ROWS


def kernel(
    q_hbm, k_hbm, v_hbm, g_hbm, doc_in, o_out, dq_out, dk_out, dv_out,
    kbuf, vbuf, dbuf, dstage, kext, qext, kt, vt, qbuf, gbuf, pbuf,
    mrow, lrow, mblk, delta, linv, ot, dqt, dkacc, dvacc, obuf, dqbuf, rbuf, sbuf, fbuf,
    xs, xr, zs, zr, rs, rr,
):
    me = lax.axis_index("sp")
    z = me // NX
    x = me % NX
    up = ((z + 1) % NZ) * NX + x
    down = ((z + NZ - 1) % NZ) * NX + x

    def peer(d):
        return (x + d) % NX

    def xid(d):
        return z * NX + peer(d)

    def cols(i, width, extra=0):
        return pl.ds(pl.multiple_of(i * width + extra, HD), width if extra == 0 else width)

    def head(h):
        return pl.ds(pl.multiple_of(h * HD, HD), HD)

    def xrefs(item, to, at):
        if item == I_K:
            return k_hbm.at[:, cols(to, HD)], kbuf.at[0, at]
        if item == I_V:
            return v_hbm.at[:, cols(to, HD)], vbuf.at[0, at]
        if item == I_DOC:
            return dstage, dbuf.at[0, at]
        if item in (I_Q0, I_Q1):
            part = (item - I_Q0) * (WIDE // 2)
            src = q_hbm.at[:, pl.ds(pl.multiple_of(to * WIDE + part, HD), WIDE // 2)]
            return src, qbuf.at[at, :, part:part + WIDE // 2]
        if item == I_G:
            return g_hbm.at[:, cols(to, WIDE)], gbuf.at[at]
        if item == I_O:
            return obuf.at[to], o_out.at[:, cols(at, WIDE)]
        if item in (I_DQ0, I_DQ1):
            part = (item - I_DQ0) * (WIDE // 2)
            dst = dq_out.at[:, pl.ds(pl.multiple_of(at * WIDE + part, HD), WIDE // 2)]
            return dqbuf.at[to, :, part:part + WIDE // 2], dst
        if item == I_DK:
            return fbuf.at[0, to], dk_out.at[:, cols(at, HD)]
        return fbuf.at[1, to], dv_out.at[:, cols(at, HD)]

    def xcopy(item, d, sending=True):
        at = x if sending else (x + NX - d) % NX
        src, dst = xrefs(item, peer(d), at)
        return pltpu.make_async_remote_copy(
            src_ref=src, dst_ref=dst, send_sem=xs.at[item, d], recv_sem=xr.at[item, d],
            device_id={"sp": xid(d)}, device_id_type=MESH,
        )

    def xlocal(item):
        src, dst = xrefs(item, x, x)
        return pltpu.make_async_copy(src, dst, xr.at[item, 0])

    def xsend(item):
        for d in (1, 3, 2):
            xcopy(item, d).start()

    def xrecv(item):
        xlocal(item).wait()
        for d in (1, 3, 2):
            xcopy(item, d, sending=False).wait_recv()

    def zcopy(far, item):
        buf = (kbuf, vbuf, dbuf)[item]
        return pltpu.make_async_remote_copy(
            src_ref=buf.at[far], dst_ref=buf.at[far + 1], send_sem=zs.at[far, item], recv_sem=zr.at[far, item],
            device_id={"sp": up}, device_id_type=MESH,
        )

    def rcopy(far, half):
        return pltpu.make_async_remote_copy(
            src_ref=sbuf.at[far - 1, half], dst_ref=rbuf.at[far - 1, half],
            send_sem=rs.at[far - 1, half], recv_sem=rr.at[far - 1, half],
            device_id={"sp": down}, device_id_type=MESH,
        )

    dstage[...] = jnp.broadcast_to(doc_in[...], (8, TOK))
    for item in (I_K, I_V, I_DOC, I_Q0, I_Q1, I_G):
        xlocal(item).start()

    barrier = pltpu.get_barrier_semaphore()
    for other in (xid(1), xid(2), xid(3), up, down):
        pl.semaphore_signal(barrier, inc=1, device_id={"sp": other}, device_id_type=MESH)
    pl.semaphore_wait(barrier, 5)

    for item in (I_K, I_V, I_DOC, I_Q0, I_Q1):
        xsend(item)

    mrow[...] = jnp.full(mrow.shape, LOW, F32)
    lrow[...] = jnp.zeros(lrow.shape, F32)

    def zero_heads(ref):
        def step(h, _):
            ref[h] = jnp.zeros((HD, ROWS), F32)
            return 0
        lax.fori_loop(0, GROUP, step, 0)

    zero_heads(ot)
    zero_heads(dqt)

    def prepare(far):
        line = lax.broadcasted_iota(jnp.int32, (TOK, TOK), 0)
        for b in range(NX):
            docs = dbuf[far, b][0:1, :]
            same = line == docs
            bias = jnp.where(same | (line >= 8), 0.0, -BIG).astype(F32)
            kext[far, b * TOK:(b + 1) * TOK, :] = bias.T.astype(BF16)
            if far == 0:
                qext[b * TOK:(b + 1) * TOK, :] = jnp.where(same, 1.0, 0.0).astype(F32).T.astype(BF16)
        for half in range(2):
            for b in range(2):
                kt[far, half, :, b * TOK:(b + 1) * TOK] = kbuf[far, 2 * half + b].astype(F32).T.astype(BF16)
                vt[far, half, :, b * TOK:(b + 1) * TOK] = vbuf[far, 2 * half + b].astype(F32).T.astype(BF16)

    def rows_in(buf, h, first, count):
        return buf[first // TOK:(first + count) // TOK, :, head(h)].reshape(count, HD)

    def over_heads(body, h0, count):
        def step(i, _):
            body([h0 + i * UNROLL + u for u in range(UNROLL)])
            return 0
        lax.fori_loop(0, count // UNROLL, step, 0)

    def forward(far, half, h0, count):
        first, rows = rows_of(far, half)
        span = slice(first, first + rows)

        def body(heads):
            keys = jnp.concatenate(
                [kbuf[far, 2 * half:2 * half + 2].reshape(HALF, HD), kext[far, half * HALF:(half + 1) * HALF, :]], axis=1
            )
            ext = qext[span, :]
            values_t = vt[far, half]
            old = [(mrow[h, :, span], lrow[h, :, span], ot[h, :, span]) for h in heads]
            scores = [dot_nt(keys, jnp.concatenate([rows_in(qbuf, h, first, rows), ext], axis=1)) for h in heads]
            if far == 0:
                key_at = lax.broadcasted_iota(jnp.int32, (HALF, rows), 0) + half * HALF
                row_at = lax.broadcasted_iota(jnp.int32, (HALF, rows), 1) + first
                scores = [jnp.where(key_at <= row_at, s, LOW) for s in scores]
            new = []
            for s, (m_old, l_old, o_old) in zip(scores, old):
                m_new = jnp.maximum(m_old, jnp.max(s, axis=0, keepdims=True))
                p = jnp.exp2((s - m_new) * (SCALE * LOG2E))
                alpha = jnp.exp2((m_old - m_new) * (SCALE * LOG2E))
                l_new = l_old * alpha + jnp.sum(p, axis=0, keepdims=True)
                pb = p.astype(BF16)
                o_new = o_old * alpha + dot_nn(values_t, pb)
                new.append((m_new, l_new, o_new, pb))
            for h, (m_new, l_new, o_new, pb) in zip(heads, new):
                mrow[h, :, span] = m_new
                mblk[far, half, h, :, span] = m_new
                lrow[h, :, span] = l_new
                ot[h, :, span] = o_new
                pbuf[far, half, h, :, span] = pb

        over_heads(body, h0, count)

    def backward(far, half, h0, count):
        first, rows = rows_of(far, half)
        span = slice(first, first + rows)

        def body(heads):
            values = vbuf[far, 2 * half:2 * half + 2].reshape(HALF, HD)
            keys_t = kt[far, half]
            grads = [rows_in(gbuf, h, first, rows) for h in heads]
            queries = [rows_in(qbuf, h, first, rows) for h in heads]
            factor = [
                jnp.exp2((mblk[far, half, h, :, span] - mrow[h, :, span]) * (SCALE * LOG2E)) * linv[h, :, span]
                for h in heads
            ]
            deltas = [delta[h, :, span] for h in heads]
            shares = [pbuf[far, half, h, :, span] for h in heads]
            dq_old = [dqt[h, :, span] for h in heads]
            pushed = [dot_nt(values, g) for g in grads]
            dv, dk, dq_new = dvacc[half], dkacc[half], []
            for i in range(len(heads)):
                w = shares[i].astype(F32) * factor[i]
                slopes = (w * (pushed[i] - deltas[i])).astype(BF16)
                dv = dv + dot_nn(w.astype(BF16), grads[i])
                dk = dk + dot_nn(slopes, queries[i])
                dq_new.append(dq_old[i] + dot_nn(keys_t, slopes))
            dvacc[half] = dv
            dkacc[half] = dk
            for h, dq in zip(heads, dq_new):
                dqt[h, :, span] = dq

        over_heads(body, h0, count)

    def pass_up(far):
        if far < FAR:
            for item in range(3):
                @pl.when(z < NZ - 1)
                def _():
                    zcopy(far, item).start()

    def arrive(far):
        for item in range(3):
            zcopy(far - 1, item).wait_recv()
            if far < FAR:
                @pl.when(z < NZ - 1)
                def _():
                    zcopy(far, item).start()

    for item in (I_K, I_V, I_DOC):
        xrecv(item)
    pass_up(0)
    prepare(0)
    xrecv(I_Q0)
    xsend(I_G)
    for half in range(2):
        forward(0, half, 0, GROUP // 2)

    @pl.when(z >= 1)
    def _():
        arrive(1)

    xrecv(I_Q1)
    for half in range(2):
        forward(0, half, GROUP // 2, GROUP // 2)
    for far in range(1, FAR + 1):
        @pl.when(z >= far)
        def _():
            if far > 1:
                arrive(far)
            prepare(far)
            for half in range(2):
                forward(far, half, 0, GROUP)

    xrecv(I_G)

    def finish(h, _):
        inverse = 1.0 / lrow[h]
        linv[h] = inverse
        out = (ot[h] * inverse).T.astype(BF16)
        obuf[:, :, head(h)] = out.reshape(NX, TOK, HD)
        prod = out.astype(F32) * rows_in(gbuf, h, 0, ROWS).astype(F32)
        high = prod.astype(BF16)
        low = (prod - high.astype(F32)).astype(BF16)
        sums = dot_nt(jnp.ones((8, 2 * HD), BF16), jnp.concatenate([high, low], axis=1))
        delta[h] = sums[0:1, :]
        return 0

    lax.fori_loop(0, GROUP, finish, 0)
    xlocal(I_O).start()
    xsend(I_O)

    def clear(half):
        dkacc[half] = jnp.zeros((HALF, HD), F32)
        dvacc[half] = jnp.zeros((HALF, HD), F32)

    def add_above(far, half):
        @pl.when(z < NZ - 1)
        def _():
            rcopy(far + 1, half).wait_recv()
            dkacc[half] = dkacc[half] + rbuf[far, half, 0].astype(F32)
            dvacc[half] = dvacc[half] + rbuf[far, half, 1].astype(F32)

    for far in range(FAR, 0, -1):
        @pl.when(z >= far)
        def _():
            for half in range(2):
                clear(half)
                backward(far, half, 0, GROUP)
                if far < FAR:
                    add_above(far, half)
                sbuf[far - 1, half, 0] = dkacc[half].astype(BF16)
                sbuf[far - 1, half, 1] = dvacc[half].astype(BF16)
                rcopy(far, half).start()

    for half in range(2):
        clear(half)
    for part in range(2):
        h0 = part * (GROUP // 2)
        for half in range(2):
            backward(0, half, h0, GROUP // 2)

        def finish_dq(i, _):
            h = h0 + i
            dq = (dqt[h] * SCALE).T.astype(BF16)
            dqbuf[:, :, head(h)] = dq.reshape(NX, TOK, HD)
            return 0

        lax.fori_loop(0, GROUP // 2, finish_dq, 0)
        xlocal(I_DQ0 + part).start()
        xsend(I_DQ0 + part)
    for half in range(2):
        add_above(0, half)
        fbuf[0, 2 * half:2 * half + 2] = (dkacc[half] * SCALE).astype(BF16).reshape(2, TOK, HD)
        fbuf[1, 2 * half:2 * half + 2] = dvacc[half].astype(BF16).reshape(2, TOK, HD)
    for item in (I_DK, I_DV):
        xlocal(item).start()
        xsend(item)

    for item in (I_O, I_DQ0, I_DQ1, I_DK, I_DV):
        xrecv(item)
    for item in range(11):
        for d in (1, 3, 2):
            xcopy(item, d).wait_send()
    for far in range(FAR):
        for item in range(3):
            @pl.when((z >= far) & (z < NZ - 1))
            def _():
                zcopy(far, item).wait_send()
    for far in range(1, FAR + 1):
        for half in range(2):
            @pl.when(z >= far)
            def _():
                rcopy(far, half).wait_send()


def per_device(query, keys, values, out_grad, documents):
    wide, narrow = query.shape, keys.shape
    hbm = pl.BlockSpec(memory_space=pl.ANY)
    vmem = pltpu.VMEM
    dma = pltpu.SemaphoreType.DMA
    return pl.pallas_call(
        kernel,
        out_shape=(
            jax.ShapeDtypeStruct(wide, BF16),
            jax.ShapeDtypeStruct(wide, BF16),
            jax.ShapeDtypeStruct(narrow, BF16),
            jax.ShapeDtypeStruct(narrow, BF16),
        ),
        in_specs=[hbm, hbm, hbm, hbm, pl.BlockSpec(memory_space=pltpu.VMEM)],
        out_specs=(hbm, hbm, hbm, hbm),
        scratch_shapes=[
            vmem((FAR + 1, NX, TOK, HD), BF16),
            vmem((FAR + 1, NX, TOK, HD), BF16),
            vmem((FAR + 1, NX, 8, TOK), jnp.int32),
            vmem((8, TOK), jnp.int32),
            vmem((FAR + 1, ROWS, HD), BF16),
            vmem((ROWS, HD), BF16),
            vmem((FAR + 1, 2, HD, HALF), BF16),
            vmem((FAR + 1, 2, HD, HALF), BF16),
            vmem((NX, TOK, WIDE), BF16),
            vmem((NX, TOK, WIDE), BF16),
            vmem((FAR + 1, 2, GROUP, HALF, ROWS), BF16),
            vmem((GROUP, 1, ROWS), F32),
            vmem((GROUP, 1, ROWS), F32),
            vmem((FAR + 1, 2, GROUP, 1, ROWS), F32),
            vmem((GROUP, 1, ROWS), F32),
            vmem((GROUP, 1, ROWS), F32),
            vmem((GROUP, HD, ROWS), F32),
            vmem((GROUP, HD, ROWS), F32),
            vmem((2, HALF, HD), F32),
            vmem((2, HALF, HD), F32),
            vmem((NX, TOK, WIDE), BF16),
            vmem((NX, TOK, WIDE), BF16),
            vmem((FAR, 2, 2, HALF, HD), BF16),
            vmem((FAR, 2, 2, HALF, HD), BF16),
            vmem((2, NX, TOK, HD), BF16),
            dma((11, NX)), dma((11, NX)),
            dma((FAR, 3)), dma((FAR, 3)),
            dma((FAR, 2)), dma((FAR, 2)),
        ],
        compiler_params=pltpu.CompilerParams(
            collective_id=0, has_side_effects=True, vmem_limit_bytes=56 * 2**20
        ),
        cost_estimate=pl.CostEstimate(flops=13 * 10**9, bytes_accessed=9 * 2**20, transcendentals=9 * 10**6),
        name="attention_both_ways",
    )(query, keys, values, out_grad, documents.reshape(1, TOK))


def solution(mesh):
    spec = P(("grp", "sp"), None)
    return jax.shard_map(
        per_device,
        mesh=mesh,
        in_specs=(spec, spec, spec, spec, P(("grp", "sp"))),
        out_specs=(spec, spec, spec, spec),
        check_vma=False,
    )
```

```python
import math

import jax
import jax.numpy as jnp
from jax import lax
from jax.experimental import pallas as pl
from jax.experimental.pallas import tpu as pltpu
from jax.sharding import PartitionSpec as P

HD = 128
TOK = 128
NX = 4
NZ = 8
GROUP = 8
ROWS = NX * TOK
HALF = ROWS // 2
FAR = 4
WIDE = GROUP * HD
UNROLL = 4
ALL = GROUP
PAD = 16
BIG = float(2**20)
LOW = -1e30
SCALE = 1.0 / math.sqrt(HD)
LOG2E = math.log2(math.e)
MESH = pl.DeviceIdType.MESH
F32, BF16 = jnp.float32, jnp.bfloat16

I_Q0, I_Q1, I_G0, I_G1, I_O0, I_O1, I_DQ0, I_DQ1, I_K, I_V, I_DOC, I_DK, I_DV = range(13)
WIDES = range(8)
ITEMS = range(13)


def dot_nt(a, b):
    return lax.dot_general(a, b, (((1,), (1,)), ((), ())), preferred_element_type=F32)


def dot_nn(a, b):
    return lax.dot_general(a, b, (((1,), (0,)), ((), ())), preferred_element_type=F32)


def kernel(
    q_hbm, k_hbm, v_hbm, g_hbm, doc_in, o_out, dq_out, dk_out, dv_out,
    kbuf, vbuf, dbuf, dstage, kext, qext, kt, vt, qbuf, gbuf, qt, gt, pbuf,
    mrow, mblk, delta, linv, ot, dqt, dkacc, dvacc, obuf, dqbuf, rbuf, sbuf, fbuf,
    xs, xr, zs, zr, rs, rr,
):
    me = lax.axis_index("sp")
    z = me // NX
    x = me % NX
    up = ((z + 1) % NZ) * NX + x
    down = ((z + NZ - 1) % NZ) * NX + x

    def peer(d):
        return (x + d) % NX

    def xid(d):
        return z * NX + peer(d)

    def cols(i, width):
        return pl.ds(pl.multiple_of(i * width, HD), width)

    def head(h):
        return pl.ds(pl.multiple_of(h * HD, HD), HD)

    def xrefs(item, to, at):
        if item in WIDES:
            part = (item % 2) * (WIDE // 2)

            def outer(ref, i):
                return ref.at[:, pl.ds(pl.multiple_of(i * WIDE + part, HD), WIDE // 2)]

            def inner(ref, i):
                return ref.at[i, :, part:part + WIDE // 2]

            if item in (I_Q0, I_Q1):
                return outer(q_hbm, to), inner(qbuf, at)
            if item in (I_G0, I_G1):
                return outer(g_hbm, to), inner(gbuf, at)
            if item in (I_O0, I_O1):
                return inner(obuf, to), outer(o_out, at)
            return inner(dqbuf, to), outer(dq_out, at)
        if item == I_K:
            return k_hbm.at[:, cols(to, HD)], kbuf.at[0, at]
        if item == I_V:
            return v_hbm.at[:, cols(to, HD)], vbuf.at[0, at]
        if item == I_DOC:
            return dstage, dbuf.at[0, at]
        if item == I_DK:
            return fbuf.at[0, to], dk_out.at[:, cols(at, HD)]
        return fbuf.at[1, to], dv_out.at[:, cols(at, HD)]

    def remote(src, dst, send, recv, other):
        return pltpu.make_async_remote_copy(
            src_ref=src, dst_ref=dst, send_sem=send, recv_sem=recv, device_id={"sp": other}, device_id_type=MESH
        )

    def xcopy(item, d, sending=True):
        src, dst = xrefs(item, peer(d), x if sending else peer(NX - d))
        return remote(src, dst, xs.at[item, d], xr.at[item, d], xid(d))

    def xlocal(item):
        src, dst = xrefs(item, x, x)
        return pltpu.make_async_copy(src, dst, xr.at[item, 0])

    def xsend(item):
        for d in (1, 3, 2):
            xcopy(item, d).start()

    def xrecv(item):
        xlocal(item).wait()
        for d in (1, 3, 2):
            xcopy(item, d, sending=False).wait_recv()

    def xsent(item):
        for d in (1, 3, 2):
            xcopy(item, d).wait_send()

    def zcopy(far, item):
        buf = (kbuf, vbuf, dbuf)[item]
        return pltpu.make_async_remote_copy(
            src_ref=buf.at[far], dst_ref=buf.at[far + 1], send_sem=zs.at[far, item], recv_sem=zr.at[far, item],
            device_id={"sp": up}, device_id_type=MESH,
        )

    def rcopy(far, half):
        return pltpu.make_async_remote_copy(
            src_ref=sbuf.at[far - 1, half], dst_ref=rbuf.at[far - 1, half],
            send_sem=rs.at[far - 1, half], recv_sem=rr.at[far - 1, half],
            device_id={"sp": down}, device_id_type=MESH,
        )

    dstage[...] = jnp.broadcast_to(doc_in[...], (8, TOK))
    for item in (I_K, I_V, I_DOC, I_Q0, I_Q1, I_G0, I_G1):
        xlocal(item).start()

    barrier = pltpu.get_barrier_semaphore()
    for other in (xid(1), xid(2), xid(3), up, down):
        pl.semaphore_signal(barrier, inc=1, device_id={"sp": other}, device_id_type=MESH)
    pl.semaphore_wait(barrier, 5)

    for item in (I_K, I_V, I_DOC):
        xsend(item)

    mrow[...] = jnp.full(mrow.shape, LOW, F32)
    for far in range(FAR + 1):
        vt[far, HD:, :] = jnp.ones((PAD, ROWS), BF16)

    def zero_head(h, _):
        ot[h] = jnp.zeros((HD + PAD, ROWS), F32)
        dqt[h] = jnp.zeros((HD, ROWS), F32)
        return 0

    lax.fori_loop(0, GROUP, zero_head, 0)

    def prepare(far):
        line = lax.broadcasted_iota(jnp.int32, (TOK, TOK), 0)
        for b in range(NX):
            bias = jnp.where((line == dbuf[far, b][0:1, :]) | (line >= 8), 0.0, -BIG).astype(F32)
            kext[far, b * TOK:(b + 1) * TOK, :] = bias.T.astype(BF16)
            kt[far, :, b * TOK:(b + 1) * TOK] = kbuf[far, b].T
            vt[far, :HD, b * TOK:(b + 1) * TOK] = vbuf[far, b].T

    def rows_in(buf, h, first, count):
        return buf[first // TOK:(first + count) // TOK, :, head(h)].reshape(count, HD)

    def turn(src, dst, h0, count):
        def step(i, _):
            for h in (h0 + 2 * i, h0 + 2 * i + 1):
                for b in range(NX):
                    dst[h, :, b * TOK:(b + 1) * TOK] = src[b, :, head(h)].T
            return 0
        lax.fori_loop(0, count // 2, step, 0)

    def over_heads(body, h0, count, together):
        def step(i, _):
            body([h0 + i * together + u for u in range(together)])
            return 0
        if count == together:
            step(0, 0)
        else:
            lax.fori_loop(0, count // together, step, 0)

    def forward(far, key0, count, first, rows, h0, heads_in, causal=False):
        span, some = slice(first, first + rows), slice(key0, key0 + count)

        def body(heads):
            keys = jnp.concatenate(
                [kbuf[far, key0 // TOK:(key0 + count) // TOK].reshape(count, HD), kext[far, some, :]], axis=1
            )
            ext = qext[:, span]
            values_t = vt[far, :, some]
            old = [(mrow[h, :, span], ot[h, :, span]) for h in heads]
            scores = [dot_nn(keys, jnp.concatenate([qt[h, :, span], ext], axis=0)) for h in heads]
            if causal:
                key_at = lax.broadcasted_iota(jnp.int32, (count, rows), 0) + key0
                row_at = lax.broadcasted_iota(jnp.int32, (count, rows), 1) + first
                scores = [jnp.where(key_at <= row_at, s, LOW) for s in scores]
            new = []
            for s, (m_old, o_old) in zip(scores, old):
                m_new = jnp.maximum(m_old, jnp.max(s, axis=0, keepdims=True))
                pb = jnp.exp2((s - m_new) * (SCALE * LOG2E)).astype(BF16)
                alpha = jnp.exp2((m_old - m_new) * (SCALE * LOG2E))
                new.append((m_new, o_old * alpha + dot_nn(values_t, pb), pb))
            for h, (m_new, o_new, pb) in zip(heads, new):
                mrow[h, :, span] = m_new
                for half in range(key0 // HALF, (key0 + count) // HALF):
                    mblk[far, half, h, :, span] = m_new
                ot[h, :, span] = o_new
                pbuf[far, h, some, span] = pb

        over_heads(body, h0, heads_in, UNROLL)

    def backward(far, half, first, rows, h0, heads_in, together):
        span = slice(first, first + rows)
        some = pl.ds(half * HALF if isinstance(half, int) else pl.multiple_of(half * HALF, HALF), HALF)

        def body(heads):
            values = vbuf[far, pl.ds(2 * half, 2)].reshape(HALF, HD)
            keys_t = kt[far, :, some]
            grads = [rows_in(gbuf, h, first, rows) for h in heads]
            queries = [rows_in(qbuf, h, first, rows) for h in heads]
            factor = [
                jnp.exp2((mblk[far, half, h, :, span] - mrow[h, :, span]) * (SCALE * LOG2E)) * linv[h, :, span]
                for h in heads
            ]
            deltas = [delta[h, :, span] for h in heads]
            shares = [pbuf[far, h, some, span] for h in heads]
            dq_old = [dqt[h, :, span] for h in heads]
            dv_old, dk_old = dvacc[half], dkacc[half]
            pushed = [dot_nn(values, gt[h, :, span]) for h in heads]
            weights, slopes, dq_new = [], [], []
            for i in range(len(heads)):
                w = shares[i].astype(F32) * factor[i]
                weights.append(w.astype(BF16))
                slopes.append((w * (pushed[i] - deltas[i])).astype(BF16))
                dq_new.append(dq_old[i] + dot_nn(keys_t, slopes[i]))
            dvacc[half] = dv_old + dot_nn(jnp.concatenate(weights, axis=1), jnp.concatenate(grads, axis=0))
            dkacc[half] = dk_old + dot_nn(jnp.concatenate(slopes, axis=1), jnp.concatenate(queries, axis=0))
            for h, dq in zip(heads, dq_new):
                dqt[h, :, span] = dq

        over_heads(body, h0, heads_in, together)

    def arrive(far, items):
        @pl.when(z >= far)
        def _():
            for item in items:
                zcopy(far - 1, item).wait_recv()

                @pl.when((far < FAR) & (z < NZ - 1))
                def _():
                    zcopy(far, item).start()

    for item in (I_K, I_V, I_DOC):
        xrecv(item)

    @pl.when(z < NZ - 1)
    def _():
        for item in range(3):
            zcopy(0, item).start()

    xsend(I_Q0)
    xsend(I_Q1)
    prepare(0)
    line = lax.broadcasted_iota(jnp.int32, (HD, TOK), 0)
    for b in range(NX):
        qext[:, b * TOK:(b + 1) * TOK] = jnp.where(line == dbuf[0, b][0:1, :], 1.0, 0.0).astype(BF16)
    arrive(1, (0, 1, 2))
    for part in range(2):
        h0 = part * (GROUP // 2)
        xrecv(I_Q0 + part)
        xsend(I_G0 + part)
        turn(qbuf, qt, h0, GROUP // 2)
        forward(0, 0, HALF, 0, ROWS, h0, GROUP // 2, causal=True)
        forward(0, HALF, HALF, HALF, HALF, h0, GROUP // 2, causal=True)

    def forward_step(i, _):
        far, part = (i + 2) // 2, i % 2

        @pl.when(part == 0)
        def _():
            arrive(far + 1, (0,))

            @pl.when(z >= far)
            def _():
                prepare(far)

        @pl.when(part == 1)
        def _():
            arrive(far + 1, (1, 2))

        @pl.when(z >= far)
        def _():
            forward(far, 0, ROWS, 0, ROWS, part * (GROUP // 2), GROUP // 2)
        return 0

    lax.fori_loop(0, 2 * (FAR - 1), forward_step, 0)

    @pl.when(z >= FAR)
    def _():
        prepare(FAR)
        forward(FAR, 0, HALF, 0, HALF, 0, GROUP)
        forward(FAR, HALF, HALF, 0, ROWS, 0, GROUP)

    xrecv(I_G0)
    xrecv(I_G1)
    turn(gbuf, gt, 0, GROUP)

    def finish(i, _):
        for h in (2 * i, 2 * i + 1):
            inverse = 1.0 / ot[h, HD:HD + 1, :]
            linv[h] = inverse
            out = (ot[h, :HD, :] * inverse).astype(BF16)
            delta[h] = jnp.sum(out.astype(F32) * gt[h].astype(F32), axis=0, keepdims=True)
            for b in range(NX):
                obuf[b, :, head(h)] = out[:, b * TOK:(b + 1) * TOK].T
        return 0

    lax.fori_loop(0, GROUP // 2, finish, 0)
    for item in (I_O0, I_O1):
        xlocal(item).start()
        xsend(item)

    def clear(half):
        dkacc[half] = jnp.zeros((HALF, HD), F32)
        dvacc[half] = jnp.zeros((HALF, HD), F32)

    def add_above(far, half):
        @pl.when(z < NZ - 1)
        def _():
            rcopy(far + 1, half).wait_recv()
            dkacc[half] = dkacc[half] + rbuf[far, half, 0].astype(F32)
            dvacc[half] = dvacc[half] + rbuf[far, half, 1].astype(F32)

    def send_down(far, half):
        sbuf[far - 1, half, 0] = dkacc[half].astype(BF16)
        sbuf[far - 1, half, 1] = dvacc[half].astype(BF16)
        rcopy(far, half).start()

    @pl.when(z >= FAR)
    def _():
        clear(0)
        backward(FAR, 0, 0, HALF, 0, GROUP, ALL)
        send_down(FAR, 0)

    def backward_step(i, _):
        far, half = (2 * FAR - i) // 2, (i + 1) % 2

        @pl.when(z >= far)
        def _():
            clear(half)
            backward(far, half, 0, ROWS, 0, GROUP, ALL)

            @pl.when((far >= 1) & (far < FAR))
            def _():
                add_above(far, half)

            @pl.when(far >= 1)
            def _():
                send_down(far, half)
        return 0

    lax.fori_loop(0, 2 * FAR, backward_step, 0)

    clear(1)
    for part in range(2):
        h0 = part * (GROUP // 2)
        backward(0, 1, HALF, HALF, h0, GROUP // 2, GROUP // 2)

        def finish_dq(i, _):
            for h in (h0 + 2 * i, h0 + 2 * i + 1):
                dq = (dqt[h] * SCALE).astype(BF16)
                for b in range(NX):
                    dqbuf[b, :, head(h)] = dq[:, b * TOK:(b + 1) * TOK].T
            return 0

        lax.fori_loop(0, GROUP // 4, finish_dq, 0)
        xlocal(I_DQ0 + part).start()
        xsend(I_DQ0 + part)
    for half in range(2):
        add_above(0, half)
        fbuf[0, 2 * half:2 * half + 2] = (dkacc[half] * SCALE).astype(BF16).reshape(2, TOK, HD)
        fbuf[1, 2 * half:2 * half + 2] = dvacc[half].astype(BF16).reshape(2, TOK, HD)
    for item in (I_DK, I_DV):
        xlocal(item).start()
        xsend(item)

    for item in (I_O0, I_O1, I_DQ0, I_DQ1, I_DK, I_DV):
        xrecv(item)
    for item in ITEMS:
        xsent(item)
    for far in range(FAR):
        @pl.when((z >= far) & (z < NZ - 1))
        def _():
            for item in range(3):
                zcopy(far, item).wait_send()
    for far in range(1, FAR + 1):
        @pl.when(z >= far)
        def _():
            for half in range(2):
                rcopy(far, half).wait_send()


def hand_over(*refs):
    sources, targets, held, sems = refs[:4], refs[4:8], refs[8:12], refs[12]
    loads = [pltpu.make_async_copy(a, b, sems.at[0, i]) for i, (a, b) in enumerate(zip(sources, held))]
    stores = [pltpu.make_async_copy(a, b, sems.at[1, i]) for i, (a, b) in enumerate(zip(held, targets))]
    for load in loads:
        load.start()
    for load, store in zip(loads, stores):
        load.wait()
        store.start()
    for store in stores:
        store.wait()


def per_device(query, keys, values, out_grad, documents):
    wide, narrow = query.shape, keys.shape
    hbm = pl.BlockSpec(memory_space=pl.ANY)
    vmem = pltpu.VMEM
    dma = pltpu.SemaphoreType.DMA
    results = pl.pallas_call(
        kernel,
        out_shape=(
            jax.ShapeDtypeStruct(wide, BF16),
            jax.ShapeDtypeStruct(wide, BF16),
            jax.ShapeDtypeStruct(narrow, BF16),
            jax.ShapeDtypeStruct(narrow, BF16),
        ),
        in_specs=[hbm, hbm, hbm, hbm, pl.BlockSpec(memory_space=pltpu.VMEM)],
        out_specs=(hbm, hbm, hbm, hbm),
        scratch_shapes=[
            vmem((FAR + 1, NX, TOK, HD), BF16),
            vmem((FAR + 1, NX, TOK, HD), BF16),
            vmem((FAR + 1, NX, 8, TOK), jnp.int32),
            vmem((8, TOK), jnp.int32),
            vmem((FAR + 1, ROWS, HD), BF16),
            vmem((HD, ROWS), BF16),
            vmem((FAR + 1, HD, ROWS), BF16),
            vmem((FAR + 1, HD + PAD, ROWS), BF16),
            vmem((NX, TOK, WIDE), BF16),
            vmem((NX, TOK, WIDE), BF16),
            vmem((GROUP, HD, ROWS), BF16),
            vmem((GROUP, HD, ROWS), BF16),
            vmem((FAR + 1, GROUP, ROWS, ROWS), BF16),
            vmem((GROUP, 1, ROWS), F32),
            vmem((FAR + 1, 2, GROUP, 1, ROWS), F32),
            vmem((GROUP, 1, ROWS), F32),
            vmem((GROUP, 1, ROWS), F32),
            vmem((GROUP, HD + PAD, ROWS), F32),
            vmem((GROUP, HD, ROWS), F32),
            vmem((2, HALF, HD), F32),
            vmem((2, HALF, HD), F32),
            vmem((NX, TOK, WIDE), BF16),
            vmem((NX, TOK, WIDE), BF16),
            vmem((FAR, 2, 2, HALF, HD), BF16),
            vmem((FAR, 2, 2, HALF, HD), BF16),
            vmem((2, NX, TOK, HD), BF16),
            dma((len(ITEMS), NX)), dma((len(ITEMS), NX)),
            dma((FAR, 3)), dma((FAR, 3)),
            dma((FAR, 2)), dma((FAR, 2)),
        ],
        compiler_params=pltpu.CompilerParams(
            collective_id=0, has_side_effects=True, vmem_limit_bytes=56 * 2**20
        ),
        cost_estimate=pl.CostEstimate(flops=13 * 10**9, bytes_accessed=9 * 2**20, transcendentals=9 * 10**6),
        name="attention_both_ways",
    )(query, keys, values, out_grad, documents.reshape(1, TOK))
    return pl.pallas_call(
        hand_over,
        out_shape=tuple(jax.ShapeDtypeStruct(r.shape, r.dtype) for r in results),
        in_specs=[hbm] * 4,
        out_specs=(hbm,) * 4,
        scratch_shapes=[vmem(r.shape, r.dtype) for r in results] + [dma((2, 4))],
        compiler_params=pltpu.CompilerParams(vmem_limit_bytes=56 * 2**20),
        cost_estimate=pl.CostEstimate(flops=0, bytes_accessed=5 * 2**20, transcendentals=0),
        name="hand_over",
    )(*results)


def solution(mesh):
    spec = P(("grp", "sp"), None)
    return jax.shard_map(
        per_device,
        mesh=mesh,
        in_specs=(spec, spec, spec, spec, P(("grp", "sp"))),
        out_specs=(spec, spec, spec, spec),
        check_vma=False,
    )
```

```python
import math

import jax
import jax.numpy as jnp
from jax import lax
from jax.experimental import pallas as pl
from jax.experimental.pallas import tpu as pltpu
from jax.sharding import PartitionSpec as P

HD = 128
TOK = 128
NX = 4
NZ = 8
GROUP = 8
ROWS = NX * TOK
HALF = ROWS // 2
FAR = 4
WIDE = GROUP * HD
UNROLL = 4
PAD = 16
BIG = float(2**20)
LOW = -1e30
SCALE = 1.0 / math.sqrt(HD)
LOG2E = math.log2(math.e)
MESH = pl.DeviceIdType.MESH
F32, BF16 = jnp.float32, jnp.bfloat16

I_Q0, I_Q1, I_G0, I_G1, I_O0, I_O1 = range(6)
I_DQ = 6
QUARTERS = 4
I_K, I_V, I_DOC, I_DK, I_DV = range(10, 15)
ITEMS = 15


def dot_nn(a, b):
    return lax.dot_general(a, b, (((1,), (0,)), ((), ())), preferred_element_type=F32)


def kernel(
    q_hbm, k_hbm, v_hbm, g_hbm, doc_in, o_out, dq_out, dk_out, dv_out,
    kbuf, vbuf, dbuf, dstage, kext, qext, kt, vt, qbuf, gbuf, qt, gt, pbuf,
    mrow, mblk, delta, linv, ot, dqt, dkacc, dvacc, obuf, dqbuf, rbuf, sbuf, fbuf,
    xs, xr, zs, zr, rs, rr,
):
    me = lax.axis_index("sp")
    z = me // NX
    x = me % NX
    up = ((z + 1) % NZ) * NX + x
    down = ((z + NZ - 1) % NZ) * NX + x

    def peer(d):
        return (x + d) % NX

    def xid(d):
        return z * NX + peer(d)

    def cols(i, width):
        return pl.ds(pl.multiple_of(i * width, HD), width)

    def head(h):
        return pl.ds(pl.multiple_of(h * HD, HD), HD)

    def xrefs(item, to, at):
        if not isinstance(item, int) or item < I_K:
            size = WIDE // 2 if isinstance(item, int) and item < I_DQ else WIDE // QUARTERS
            part = pl.multiple_of((item - I_DQ) * size, HD) if size != WIDE // 2 else (item % 2) * size

            def outer(ref, i):
                return ref.at[:, pl.ds(pl.multiple_of(i * WIDE + part, HD), size)]

            def inner(ref, i):
                return ref.at[i, :, pl.ds(part, size)]

            if size != WIDE // 2:
                return inner(dqbuf, to), outer(dq_out, at)
            if item in (I_Q0, I_Q1):
                return outer(q_hbm, to), inner(qbuf, at)
            if item in (I_G0, I_G1):
                return outer(g_hbm, to), inner(gbuf, at)
            return inner(obuf, to), outer(o_out, at)
        if item == I_K:
            return k_hbm.at[:, cols(to, HD)], kbuf.at[0, at]
        if item == I_V:
            return v_hbm.at[:, cols(to, HD)], vbuf.at[0, at]
        if item == I_DOC:
            return dstage, dbuf.at[0, at]
        if item == I_DK:
            return fbuf.at[0, to], dk_out.at[:, cols(at, HD)]
        return fbuf.at[1, to], dv_out.at[:, cols(at, HD)]

    def remote(src, dst, send, recv, other):
        return pltpu.make_async_remote_copy(
            src_ref=src, dst_ref=dst, send_sem=send, recv_sem=recv, device_id={"sp": other}, device_id_type=MESH
        )

    def xcopy(item, d, sending=True):
        src, dst = xrefs(item, peer(d), x if sending else peer(NX - d))
        return remote(src, dst, xs.at[item, d], xr.at[item, d], xid(d))

    def xlocal(item):
        src, dst = xrefs(item, x, x)
        return pltpu.make_async_copy(src, dst, xr.at[item, 0])

    def xsend(item):
        for d in (1, 3, 2):
            xcopy(item, d).start()

    def xrecv(item):
        xlocal(item).wait()
        for d in (1, 3, 2):
            xcopy(item, d, sending=False).wait_recv()

    def xsent(item):
        for d in (1, 3, 2):
            xcopy(item, d).wait_send()

    def zcopy(far, item):
        buf = (kbuf, vbuf, dbuf)[item]
        return pltpu.make_async_remote_copy(
            src_ref=buf.at[far], dst_ref=buf.at[far + 1], send_sem=zs.at[far, item], recv_sem=zr.at[far, item],
            device_id={"sp": up}, device_id_type=MESH,
        )

    def rcopy(far, half):
        return pltpu.make_async_remote_copy(
            src_ref=sbuf.at[far - 1, half], dst_ref=rbuf.at[far - 1, half],
            send_sem=rs.at[far - 1, half], recv_sem=rr.at[far - 1, half],
            device_id={"sp": down}, device_id_type=MESH,
        )

    dstage[...] = jnp.broadcast_to(doc_in[...], (8, TOK))
    for item in (I_K, I_V, I_DOC, I_Q0, I_Q1, I_G0, I_G1):
        xlocal(item).start()

    barrier = pltpu.get_barrier_semaphore()
    for other in (xid(1), xid(2), xid(3), up, down):
        pl.semaphore_signal(barrier, inc=1, device_id={"sp": other}, device_id_type=MESH)
    pl.semaphore_wait(barrier, 5)

    for item in (I_K, I_V, I_DOC):
        xsend(item)

    mrow[...] = jnp.full(mrow.shape, LOW, F32)
    for far in range(FAR + 1):
        vt[far, HD:, :] = jnp.ones((PAD, ROWS), BF16)

    def zero_head(h, _):
        ot[h] = jnp.zeros((HD + PAD, ROWS), F32)
        dqt[h] = jnp.zeros((HD, ROWS), F32)
        return 0

    lax.fori_loop(0, GROUP, zero_head, 0)

    def prepare(far):
        line = lax.broadcasted_iota(jnp.int32, (TOK, TOK), 0)
        for b in range(NX):
            bias = jnp.where((line == dbuf[far, b][0:1, :]) | (line >= 8), 0.0, -BIG).astype(F32)
            kext[far, b * TOK:(b + 1) * TOK, :] = bias.T.astype(BF16)
            kt[far, :, b * TOK:(b + 1) * TOK] = kbuf[far, b].T
            vt[far, :HD, b * TOK:(b + 1) * TOK] = vbuf[far, b].T

    def rows_in(buf, h, first, count):
        return buf[first // TOK:(first + count) // TOK, :, head(h)].reshape(count, HD)

    def turn(src, dst, h0, count):
        def step(i, _):
            for h in (h0 + 2 * i, h0 + 2 * i + 1):
                for b in range(NX):
                    dst[h, :, b * TOK:(b + 1) * TOK] = src[b, :, head(h)].T
            return 0
        lax.fori_loop(0, count // 2, step, 0)

    def over_heads(body, h0, count, together):
        def step(i, _):
            body([h0 + i * together + u for u in range(together)])
            return 0
        if count == together:
            step(0, 0)
        else:
            lax.fori_loop(0, count // together, step, 0)

    def forward(far, key0, count, first, rows, h0, heads_in, causal=False):
        span, some = slice(first, first + rows), slice(key0, key0 + count)

        def body(heads):
            keys = jnp.concatenate(
                [kbuf[far, key0 // TOK:(key0 + count) // TOK].reshape(count, HD), kext[far, some, :]], axis=1
            )
            ext = qext[:, span]
            values_t = vt[far, :, some]
            old = [(mrow[h, :, span], ot[h, :, span]) for h in heads]
            scores = [dot_nn(keys, jnp.concatenate([qt[h, :, span], ext], axis=0)) for h in heads]
            if causal:
                key_at = lax.broadcasted_iota(jnp.int32, (count, rows), 0) + key0
                row_at = lax.broadcasted_iota(jnp.int32, (count, rows), 1) + first
                scores = [jnp.where(key_at <= row_at, s, LOW) for s in scores]
            new = []
            for s, (m_old, o_old) in zip(scores, old):
                m_new = jnp.maximum(m_old, jnp.max(s, axis=0, keepdims=True))
                pb = jnp.exp2((s - m_new) * (SCALE * LOG2E)).astype(BF16)
                alpha = jnp.exp2((m_old - m_new) * (SCALE * LOG2E))
                new.append((m_new, o_old * alpha + dot_nn(values_t, pb), pb))
            for h, (m_new, o_new, pb) in zip(heads, new):
                mrow[h, :, span] = m_new
                for half in range(key0 // HALF, (key0 + count) // HALF):
                    mblk[far, half, h, :, span] = m_new
                ot[h, :, span] = o_new
                pbuf[far, h, some, span] = pb

        over_heads(body, h0, heads_in, UNROLL)

    def gradients(tiles, heads):
        loaded = []
        for far, half, first, rows, slot in tiles:
            span = slice(first, first + rows)
            some = pl.ds(half * HALF if isinstance(half, int) else pl.multiple_of(half * HALF, HALF), HALF)
            loaded.append((
                vbuf[far, pl.ds(2 * half, 2)].reshape(HALF, HD),
                kt[far, :, some],
                [(jnp.exp2((mblk[far, half, h, :, span] - mrow[h, :, span]) * (SCALE * LOG2E)) * linv[h, :, span]
                  ).astype(BF16) for h in heads],
                [pbuf[far, h, some, span] for h in heads],
                dvacc[slot], dkacc[slot],
            ))
        grads = [rows_in(gbuf, h, 0, ROWS) for h in heads]
        queries = [rows_in(qbuf, h, 0, ROWS) for h in heads]
        grads_t = [gt[h] for h in heads]
        deltas = [delta[h] for h in heads]
        dq = [dqt[h] for h in heads]
        pushed = [
            [dot_nn(t[0], g[:, first:first + rows]) for g in grads_t]
            for t, (_, _, first, rows, _) in zip(loaded, tiles)
        ]
        sums = []
        for t, pushes, (_, _, first, rows, _) in zip(loaded, pushed, tiles):
            _, keys_t, factor, shares, dv_old, dk_old = t
            span = slice(first, first + rows)
            weights, slopes = [], []
            for i in range(len(heads)):
                weights.append(shares[i] * factor[i])
                slopes.append(weights[i] * (pushes[i] - deltas[i][:, span]).astype(BF16))
                term = dot_nn(keys_t, slopes[i])
                parts = [dq[i][:, :first]] if first else []
                parts.append(dq[i][:, span] + term)
                if first + rows < ROWS:
                    parts.append(dq[i][:, first + rows:])
                dq[i] = parts[0] if len(parts) == 1 else jnp.concatenate(parts, axis=1)
            sums.append((
                dv_old + dot_nn(jnp.concatenate(weights, axis=1), jnp.concatenate([g[span] for g in grads], axis=0)),
                dk_old + dot_nn(jnp.concatenate(slopes, axis=1), jnp.concatenate([q[span] for q in queries], axis=0)),
            ))
        for (_, _, _, _, slot), (dv, dk) in zip(tiles, sums):
            dvacc[slot] = dv
            dkacc[slot] = dk
        return dq

    def backward(far, half, first, rows, heads):
        for h, dq in zip(heads, gradients([(far, half, first, rows, half)], heads)):
            dqt[h] = dq

    def arrive(far, items):
        @pl.when(z >= far)
        def _():
            for item in items:
                zcopy(far - 1, item).wait_recv()

                if not (isinstance(far, int) and far == FAR):
                    @pl.when(z < NZ - 1)
                    def _():
                        zcopy(far, item).start()

    for item, own in enumerate((I_K, I_V, I_DOC)):
        xrecv(own)

        @pl.when(z < NZ - 1)
        def _():
            zcopy(0, item).start()

    xsend(I_Q0)
    prepare(0)
    line = lax.broadcasted_iota(jnp.int32, (HD, TOK), 0)
    for b in range(NX):
        qext[:, b * TOK:(b + 1) * TOK] = jnp.where(line == dbuf[0, b][0:1, :], 1.0, 0.0).astype(BF16)
    arrive(1, (0, 1, 2))

    def own_row(part):
        h0 = part * (GROUP // 2)
        xrecv(I_Q0 + part)
        if part == 0:
            xsend(I_Q1)
        else:
            xsend(I_G0)
            xsend(I_G1)
        turn(qbuf, qt, h0, GROUP // 2)
        forward(0, 0, HALF, 0, ROWS, h0, GROUP // 2, causal=True)
        forward(0, HALF, HALF, HALF, HALF, h0, GROUP // 2, causal=True)

    own_row(0)

    def forward_step(i, _):
        late = i // 4
        far = (1 - late) * (1 + i % 2) + late * 3
        part = (1 - late) * (i // 2) + late * (i - 4)

        @pl.when(i == 0)
        def _():
            arrive(2, (0,))

        @pl.when(i == 1)
        def _():
            arrive(2, (1, 2))

        @pl.when(i == 2)
        def _():
            arrive(3, (0,))
            own_row(1)
            arrive(3, (1, 2))

        @pl.when(((i < 2) | (i == 4)) & (z >= far))
        def _():
            prepare(far)

        @pl.when(z >= far)
        def _():
            forward(far, 0, ROWS, 0, ROWS, part * (GROUP // 2), GROUP // 2)
        return 0

    lax.fori_loop(0, 2 * (FAR - 1), forward_step, 0)
    xrecv(I_G0)
    turn(gbuf, gt, 0, GROUP // 2)
    arrive(FAR, (0, 1, 2))

    @pl.when(z >= FAR)
    def _():
        prepare(FAR)
        forward(FAR, 0, HALF, 0, HALF, 0, GROUP)
        forward(FAR, HALF, HALF, 0, ROWS, 0, GROUP)

    xrecv(I_G1)
    turn(gbuf, gt, GROUP // 2, GROUP // 2)

    def finish(i, _):
        for h in [4 * i + u for u in range(4)]:
            inverse = 1.0 / ot[h, HD:HD + 1, :]
            linv[h] = inverse
            out = (ot[h, :HD, :] * inverse).astype(BF16)
            delta[h] = jnp.sum(out.astype(F32) * gt[h].astype(F32), axis=0, keepdims=True)
            for b in range(NX):
                obuf[b, :, head(h)] = out[:, b * TOK:(b + 1) * TOK].T
        return 0

    lax.fori_loop(0, GROUP // 4, finish, 0)
    for item in (I_O0, I_O1):
        xlocal(item).start()
        xsend(item)

    everyone = list(range(GROUP))

    def clear(slot):
        dkacc[slot] = jnp.zeros((HALF, HD), F32)
        dvacc[slot] = jnp.zeros((HALF, HD), F32)

    def add_above(far, half, slot):
        @pl.when(z < NZ - 1)
        def _():
            rcopy(far + 1, half).wait_recv()
            dkacc[slot] = dkacc[slot] + rbuf[far, half, 0].astype(F32)
            dvacc[slot] = dvacc[slot] + rbuf[far, half, 1].astype(F32)

    def send_down(far, half):
        sbuf[far - 1, half, 0] = dkacc[half].astype(BF16)
        sbuf[far - 1, half, 1] = dvacc[half].astype(BF16)
        rcopy(far, half).start()

    @pl.when(z >= FAR)
    def _():
        clear(0)
        backward(FAR, 0, 0, HALF, everyone)
        send_down(FAR, 0)

    def backward_step(i, _):
        far, half = (2 * FAR - i) // 2, (i + 1) % 2

        @pl.when(z >= far)
        def _():
            clear(half)
            backward(far, half, 0, ROWS, everyone)

            @pl.when(far < FAR)
            def _():
                add_above(far, half, half)

            send_down(far, half)
        return 0

    lax.fori_loop(0, 2 * FAR - 2, backward_step, 0)

    for slot in (1, 2, 3):
        clear(slot)
    last = (1, 1, 0, ROWS, 1)
    own = [(0, 0, 0, ROWS, 2), (0, 1, HALF, HALF, 3)]
    pair = GROUP // QUARTERS

    def finish_dq(g, tiles):
        heads = [g * pair + u for u in range(pair)]
        for h, dq in zip(heads, gradients(tiles, heads)):
            dq = (dq * SCALE).astype(BF16)
            for b in range(NX):
                dqbuf[b, :, head(h)] = dq[:, b * TOK:(b + 1) * TOK].T
        xlocal(I_DQ + g).start()
        xsend(I_DQ + g)

    @pl.when(z >= 1)
    def _():
        def step(g, _):
            finish_dq(g, [last] + own)
            return 0
        lax.fori_loop(0, QUARTERS - 1, step, 0)
        backward(1, 1, 0, ROWS, everyone[-pair:])
        add_above(1, 1, 1)
        send_down(1, 1)

    @pl.when(z == 0)
    def _():
        def step(g, _):
            finish_dq(g, own)
            return 0
        lax.fori_loop(0, QUARTERS - 1, step, 0)

    finish_dq(QUARTERS - 1, own)
    for half in range(2):
        add_above(0, half, 2 + half)
        fbuf[0, 2 * half:2 * half + 2] = (dkacc[2 + half] * SCALE).astype(BF16).reshape(2, TOK, HD)
        fbuf[1, 2 * half:2 * half + 2] = dvacc[2 + half].astype(BF16).reshape(2, TOK, HD)
        for item in (I_DK, I_DV):
            @pl.when(x // 2 == half)
            def _():
                xlocal(item).start()
            for d in (1, 3, 2):
                @pl.when(peer(d) // 2 == half)
                def _():
                    xcopy(item, d).start()

    for item in [I_O0, I_O1, I_DK, I_DV] + [I_DQ + g for g in range(QUARTERS)]:
        xrecv(item)
    for item in range(ITEMS):
        xsent(item)
    for far in range(FAR):
        @pl.when((z >= far) & (z < NZ - 1))
        def _():
            for item in range(3):
                zcopy(far, item).wait_send()
    for far in range(1, FAR + 1):
        @pl.when(z >= far)
        def _():
            for half in range(2):
                rcopy(far, half).wait_send()


def hand_over(*refs):
    sources, targets, held, sems = refs[:4], refs[4:8], refs[8:12], refs[12]
    loads = [pltpu.make_async_copy(a, b, sems.at[0, i]) for i, (a, b) in enumerate(zip(sources, held))]
    stores = [pltpu.make_async_copy(a, b, sems.at[1, i]) for i, (a, b) in enumerate(zip(held, targets))]
    for load in loads:
        load.start()
    for load, store in zip(loads, stores):
        load.wait()
        store.start()
    for store in stores:
        store.wait()


def per_device(query, keys, values, out_grad, documents):
    wide, narrow = query.shape, keys.shape
    hbm = pl.BlockSpec(memory_space=pl.ANY)
    vmem = pltpu.VMEM
    dma = pltpu.SemaphoreType.DMA
    results = pl.pallas_call(
        kernel,
        out_shape=(
            jax.ShapeDtypeStruct(wide, BF16),
            jax.ShapeDtypeStruct(wide, BF16),
            jax.ShapeDtypeStruct(narrow, BF16),
            jax.ShapeDtypeStruct(narrow, BF16),
        ),
        in_specs=[hbm, hbm, hbm, hbm, pl.BlockSpec(memory_space=pltpu.VMEM)],
        out_specs=(hbm, hbm, hbm, hbm),
        scratch_shapes=[
            vmem((FAR + 1, NX, TOK, HD), BF16),
            vmem((FAR + 1, NX, TOK, HD), BF16),
            vmem((FAR + 1, NX, 8, TOK), jnp.int32),
            vmem((8, TOK), jnp.int32),
            vmem((FAR + 1, ROWS, HD), BF16),
            vmem((HD, ROWS), BF16),
            vmem((FAR + 1, HD, ROWS), BF16),
            vmem((FAR + 1, HD + PAD, ROWS), BF16),
            vmem((NX, TOK, WIDE), BF16),
            vmem((NX, TOK, WIDE), BF16),
            vmem((GROUP, HD, ROWS), BF16),
            vmem((GROUP, HD, ROWS), BF16),
            vmem((FAR + 1, GROUP, ROWS, ROWS), BF16),
            vmem((GROUP, 1, ROWS), F32),
            vmem((FAR + 1, 2, GROUP, 1, ROWS), F32),
            vmem((GROUP, 1, ROWS), F32),
            vmem((GROUP, 1, ROWS), F32),
            vmem((GROUP, HD + PAD, ROWS), F32),
            vmem((GROUP, HD, ROWS), F32),
            vmem((4, HALF, HD), F32),
            vmem((4, HALF, HD), F32),
            vmem((NX, TOK, WIDE), BF16),
            vmem((NX, TOK, WIDE), BF16),
            vmem((FAR, 2, 2, HALF, HD), BF16),
            vmem((FAR, 2, 2, HALF, HD), BF16),
            vmem((2, NX, TOK, HD), BF16),
            dma((ITEMS, NX)), dma((ITEMS, NX)),
            dma((FAR, 3)), dma((FAR, 3)),
            dma((FAR, 2)), dma((FAR, 2)),
        ],
        compiler_params=pltpu.CompilerParams(
            collective_id=0, has_side_effects=True, vmem_limit_bytes=56 * 2**20
        ),
        cost_estimate=pl.CostEstimate(flops=13 * 10**9, bytes_accessed=9 * 2**20, transcendentals=9 * 10**6),
        name="attention_both_ways",
    )(query, keys, values, out_grad, documents.reshape(1, TOK))
    return pl.pallas_call(
        hand_over,
        out_shape=tuple(jax.ShapeDtypeStruct(r.shape, r.dtype) for r in results),
        in_specs=[hbm] * 4,
        out_specs=(hbm,) * 4,
        scratch_shapes=[vmem(r.shape, r.dtype) for r in results] + [dma((2, 4))],
        compiler_params=pltpu.CompilerParams(vmem_limit_bytes=56 * 2**20),
        cost_estimate=pl.CostEstimate(flops=0, bytes_accessed=5 * 2**20, transcendentals=0),
        name="hand_over",
    )(*results)


def solution(mesh):
    spec = P(("grp", "sp"), None)
    return jax.shard_map(
        per_device,
        mesh=mesh,
        in_specs=(spec, spec, spec, spec, P(("grp", "sp"))),
        out_specs=(spec, spec, spec, spec),
        check_vma=False,
    )
```

```python
import math

import jax
import jax.numpy as jnp
from jax import lax
from jax.experimental import pallas as pl
from jax.experimental.pallas import tpu as pltpu
from jax.sharding import PartitionSpec as P

HD = 128
TOK = 128
NX = 4
NZ = 8
GROUP = 8
ROWS = NX * TOK
HALF = ROWS // 2
FAR = 4
WIDE = GROUP * HD
UNROLL = 4
PAD = 16
BIG = float(2**20)
LOW = -1e30
SCALE = 1.0 / math.sqrt(HD)
LOG2E = math.log2(math.e)
MESH = pl.DeviceIdType.MESH
F32, BF16 = jnp.float32, jnp.bfloat16

I_Q0, I_Q1, I_G0, I_G1, I_O0, I_O1 = range(6)
I_DQ = 6
QUARTERS = 4
I_K, I_V, I_DOC, I_DK, I_DV = range(10, 15)
ITEMS = 15


def dot_nn(a, b):
    return lax.dot_general(a, b, (((1,), (0,)), ((), ())), preferred_element_type=F32)


def kernel(
    q_hbm, k_hbm, v_hbm, g_hbm, doc_in, o_out, dq_out, dk_out, dv_out,
    kbuf, vbuf, dbuf, dstage, kext, qext, kt, vt, qbuf, gbuf, qt, gt, pbuf,
    mrow, mblk, delta, linv, ot, dqt, dkacc, dvacc, obuf, dqbuf, rbuf, sbuf, fbuf,
    xs, xr, zs, zr, rs, rr,
):
    me = lax.axis_index("sp")
    z = me // NX
    x = me % NX
    up = ((z + 1) % NZ) * NX + x
    down = ((z + NZ - 1) % NZ) * NX + x

    def peer(d):
        return (x + d) % NX

    def xid(d):
        return z * NX + peer(d)

    def cols(i, width):
        return pl.ds(pl.multiple_of(i * width, HD), width)

    def head(h):
        return pl.ds(pl.multiple_of(h * HD, HD), HD)

    def xrefs(item, to, at):
        if not isinstance(item, int) or item < I_K:
            size = WIDE // 2 if isinstance(item, int) and item < I_DQ else WIDE // QUARTERS
            part = pl.multiple_of((item - I_DQ) * size, HD) if size != WIDE // 2 else (item % 2) * size

            def outer(ref, i):
                return ref.at[:, pl.ds(pl.multiple_of(i * WIDE + part, HD), size)]

            def inner(ref, i):
                return ref.at[i, :, pl.ds(part, size)]

            if size != WIDE // 2:
                return inner(dqbuf, to), outer(dq_out, at)
            if item in (I_Q0, I_Q1):
                return outer(q_hbm, to), inner(qbuf, at)
            if item in (I_G0, I_G1):
                return outer(g_hbm, to), inner(gbuf, at)
            return inner(obuf, to), outer(o_out, at)
        if item == I_K:
            return k_hbm.at[:, cols(to, HD)], kbuf.at[0, at]
        if item == I_V:
            return v_hbm.at[:, cols(to, HD)], vbuf.at[0, at]
        if item == I_DOC:
            return dstage, dbuf.at[0, at]
        if item == I_DK:
            return fbuf.at[0, to], dk_out.at[:, cols(at, HD)]
        return fbuf.at[1, to], dv_out.at[:, cols(at, HD)]

    def remote(src, dst, send, recv, other):
        return pltpu.make_async_remote_copy(
            src_ref=src, dst_ref=dst, send_sem=send, recv_sem=recv, device_id={"sp": other}, device_id_type=MESH
        )

    def xcopy(item, d, sending=True):
        src, dst = xrefs(item, peer(d), x if sending else peer(NX - d))
        return remote(src, dst, xs.at[item, d], xr.at[item, d], xid(d))

    def xlocal(item):
        src, dst = xrefs(item, x, x)
        return pltpu.make_async_copy(src, dst, xr.at[item, 0])

    def xsend(item):
        for d in (1, 3, 2):
            xcopy(item, d).start()

    def xrecv(item):
        xlocal(item).wait()
        for d in (1, 3, 2):
            xcopy(item, d, sending=False).wait_recv()

    def xsent(item):
        for d in (1, 3, 2):
            xcopy(item, d).wait_send()

    def zcopy(far, item):
        buf = (kbuf, vbuf, dbuf)[item]
        return pltpu.make_async_remote_copy(
            src_ref=buf.at[far], dst_ref=buf.at[far + 1], send_sem=zs.at[far, item], recv_sem=zr.at[far, item],
            device_id={"sp": up}, device_id_type=MESH,
        )

    def rcopy(far, half):
        return pltpu.make_async_remote_copy(
            src_ref=sbuf.at[far - 1, half], dst_ref=rbuf.at[far - 1, half],
            send_sem=rs.at[far - 1, half], recv_sem=rr.at[far - 1, half],
            device_id={"sp": down}, device_id_type=MESH,
        )

    dstage[...] = jnp.broadcast_to(doc_in[...], (8, TOK))
    for item in (I_K, I_V, I_DOC, I_Q0, I_Q1, I_G0, I_G1):
        xlocal(item).start()

    barrier = pltpu.get_barrier_semaphore()
    for other in (xid(1), xid(2), xid(3), up, down):
        pl.semaphore_signal(barrier, inc=1, device_id={"sp": other}, device_id_type=MESH)
    pl.semaphore_wait(barrier, 5)

    for item in (I_K, I_V, I_DOC):
        xsend(item)

    mrow[...] = jnp.full(mrow.shape, LOW, F32)
    for far in range(FAR + 1):
        vt[far, HD:, :] = jnp.ones((PAD, ROWS), BF16)

    def zero_head(h, _):
        ot[h] = jnp.zeros((HD + PAD, ROWS), F32)
        dqt[h] = jnp.zeros((HD, ROWS), F32)
        return 0

    lax.fori_loop(0, GROUP, zero_head, 0)

    def prepare(far):
        line = lax.broadcasted_iota(jnp.int32, (TOK, TOK), 0)
        for b in range(NX):
            bias = jnp.where((line == dbuf[far, b][0:1, :]) | (line >= 8), 0.0, -BIG).astype(F32)
            kext[far, b * TOK:(b + 1) * TOK, :] = bias.T.astype(BF16)
            kt[far, :, b * TOK:(b + 1) * TOK] = kbuf[far, b].T
            vt[far, :HD, b * TOK:(b + 1) * TOK] = vbuf[far, b].T

    def rows_in(buf, h, first, count):
        return buf[first // TOK:(first + count) // TOK, :, head(h)].reshape(count, HD)

    def turn(src, dst, h0, count):
        def step(i, _):
            for h in (h0 + 2 * i, h0 + 2 * i + 1):
                for b in range(NX):
                    dst[h, :, b * TOK:(b + 1) * TOK] = src[b, :, head(h)].T
            return 0
        lax.fori_loop(0, count // 2, step, 0)

    def over_heads(body, h0, count, together):
        def step(i, _):
            body([h0 + i * together + u for u in range(together)])
            return 0
        if count == together:
            step(0, 0)
        else:
            lax.fori_loop(0, count // together, step, 0)

    def forward(far, key0, count, first, rows, h0, heads_in, causal=False):
        span, some = slice(first, first + rows), slice(key0, key0 + count)

        def body(heads):
            keys = jnp.concatenate(
                [kbuf[far, key0 // TOK:(key0 + count) // TOK].reshape(count, HD), kext[far, some, :]], axis=1
            )
            ext = qext[:, span]
            values_t = vt[far, :, some]
            old = [(mrow[h, :, span], ot[h, :, span]) for h in heads]
            scores = [dot_nn(keys, jnp.concatenate([qt[h, :, span], ext], axis=0)) for h in heads]
            if causal:
                key_at = lax.broadcasted_iota(jnp.int32, (count, rows), 0) + key0
                row_at = lax.broadcasted_iota(jnp.int32, (count, rows), 1) + first
                scores = [jnp.where(key_at <= row_at, s, LOW) for s in scores]
            new = []
            for s, (m_old, o_old) in zip(scores, old):
                m_new = jnp.maximum(m_old, jnp.max(s, axis=0, keepdims=True))
                pb = jnp.exp2((s - m_new) * (SCALE * LOG2E)).astype(BF16)
                alpha = jnp.exp2((m_old - m_new) * (SCALE * LOG2E))
                new.append((m_new, o_old * alpha + dot_nn(values_t, pb), pb))
            for h, (m_new, o_new, pb) in zip(heads, new):
                mrow[h, :, span] = m_new
                for half in range(key0 // HALF, (key0 + count) // HALF):
                    mblk[far, half, h, :, span] = m_new
                ot[h, :, span] = o_new
                pbuf[far, h, some, span] = pb

        over_heads(body, h0, heads_in, UNROLL)

    def gradients(tiles, heads):
        loaded = []
        for far, half, first, rows, slot in tiles:
            span = slice(first, first + rows)
            some = pl.ds(half * HALF if isinstance(half, int) else pl.multiple_of(half * HALF, HALF), HALF)
            loaded.append((
                vbuf[far, pl.ds(2 * half, 2)].reshape(HALF, HD),
                kt[far, :, some],
                [(jnp.exp2((mblk[far, half, h, :, span] - mrow[h, :, span]) * (SCALE * LOG2E)) * linv[h, :, span]
                  ).astype(BF16) for h in heads],
                [pbuf[far, h, some, span] for h in heads],
                dvacc[slot], dkacc[slot],
            ))
        grads = [rows_in(gbuf, h, 0, ROWS) for h in heads]
        queries = [rows_in(qbuf, h, 0, ROWS) for h in heads]
        grads_t = [gt[h] for h in heads]
        deltas = [delta[h] for h in heads]
        dq = [dqt[h] for h in heads]
        units = [(t, pair) for t in range(len(tiles)) for pair in zip(range(0, len(heads), 2), range(1, len(heads), 2))]

        def push(unit):
            t, pair = unit
            _, _, first, rows, _ = tiles[t]
            return [dot_nn(loaded[t][0], grads_t[i][:, first:first + rows]) for i in pair]

        sums = [(t[4], t[5]) for t in loaded]
        pushed = [push(unit) for unit in units[:2]]
        for n, (t, pair) in enumerate(units):
            _, keys_t, factor, shares, _, _ = loaded[t]
            _, _, first, rows, _ = tiles[t]
            span = slice(first, first + rows)
            weights, slopes = [], []
            for i, pushes in zip(pair, pushed[n]):
                w = shares[i] * factor[i]
                weights.append(w)
                slopes.append(w * (pushes - deltas[i][:, span]).astype(BF16))
            if n + 2 < len(units):
                pushed.append(push(units[n + 2]))
            for i, slope in zip(pair, slopes):
                parts = [dq[i][:, :first]] if first else []
                parts.append(dq[i][:, span] + dot_nn(keys_t, slope))
                if first + rows < ROWS:
                    parts.append(dq[i][:, first + rows:])
                dq[i] = parts[0] if len(parts) == 1 else jnp.concatenate(parts, axis=1)
            dv, dk = sums[t]
            sums[t] = (
                dv + dot_nn(jnp.concatenate(weights, axis=1), jnp.concatenate([grads[i][span] for i in pair], axis=0)),
                dk + dot_nn(jnp.concatenate(slopes, axis=1), jnp.concatenate([queries[i][span] for i in pair], axis=0)),
            )
        for (_, _, _, _, slot), (dv, dk) in zip(tiles, sums):
            dvacc[slot] = dv
            dkacc[slot] = dk
        return dq

    def backward(far, half, first, rows, heads):
        for h, dq in zip(heads, gradients([(far, half, first, rows, half)], heads)):
            dqt[h] = dq

    def arrive(far, items):
        @pl.when(z >= far)
        def _():
            for item in items:
                zcopy(far - 1, item).wait_recv()

                if not (isinstance(far, int) and far == FAR):
                    @pl.when(z < NZ - 1)
                    def _():
                        zcopy(far, item).start()

    for item, own in enumerate((I_K, I_V, I_DOC)):
        xrecv(own)

        @pl.when(z < NZ - 1)
        def _():
            zcopy(0, item).start()

    xsend(I_Q0)
    prepare(0)
    line = lax.broadcasted_iota(jnp.int32, (HD, TOK), 0)
    for b in range(NX):
        qext[:, b * TOK:(b + 1) * TOK] = jnp.where(line == dbuf[0, b][0:1, :], 1.0, 0.0).astype(BF16)
    arrive(1, (0, 1, 2))

    def own_row(part):
        h0 = part * (GROUP // 2)
        xrecv(I_Q0 + part)
        if part == 0:
            xsend(I_Q1)
        else:
            xsend(I_G0)
            xsend(I_G1)
        turn(qbuf, qt, h0, GROUP // 2)
        forward(0, 0, HALF, 0, ROWS, h0, GROUP // 2, causal=True)
        forward(0, HALF, HALF, HALF, HALF, h0, GROUP // 2, causal=True)

    own_row(0)

    def forward_step(i, _):
        late = i // 4
        far = (1 - late) * (1 + i % 2) + late * 3
        part = (1 - late) * (i // 2) + late * (i - 4)

        @pl.when(i == 0)
        def _():
            arrive(2, (0,))

        @pl.when(i == 1)
        def _():
            arrive(2, (1, 2))

        @pl.when(i == 2)
        def _():
            arrive(3, (0,))
            own_row(1)
            arrive(3, (1, 2))

        @pl.when(((i < 2) | (i == 4)) & (z >= far))
        def _():
            prepare(far)

        @pl.when(z >= far)
        def _():
            forward(far, 0, ROWS, 0, ROWS, part * (GROUP // 2), GROUP // 2)
        return 0

    lax.fori_loop(0, 2 * (FAR - 1), forward_step, 0)
    xrecv(I_G0)
    turn(gbuf, gt, 0, GROUP // 2)
    arrive(FAR, (0, 1, 2))

    @pl.when(z >= FAR)
    def _():
        prepare(FAR)
        forward(FAR, 0, HALF, 0, HALF, 0, GROUP)
        forward(FAR, HALF, HALF, 0, ROWS, 0, GROUP)

    xrecv(I_G1)
    turn(gbuf, gt, GROUP // 2, GROUP // 2)

    def finish(i, _):
        for h in [4 * i + u for u in range(4)]:
            inverse = 1.0 / ot[h, HD:HD + 1, :]
            linv[h] = inverse
            out = (ot[h, :HD, :] * inverse).astype(BF16)
            delta[h] = jnp.sum(out.astype(F32) * gt[h].astype(F32), axis=0, keepdims=True)
            for b in range(NX):
                obuf[b, :, head(h)] = out[:, b * TOK:(b + 1) * TOK].T
        return 0

    lax.fori_loop(0, GROUP // 4, finish, 0)
    for item in (I_O0, I_O1):
        xlocal(item).start()
        xsend(item)

    everyone = list(range(GROUP))

    def clear(slot):
        dkacc[slot] = jnp.zeros((HALF, HD), F32)
        dvacc[slot] = jnp.zeros((HALF, HD), F32)

    def add_above(far, half, slot):
        @pl.when(z < NZ - 1)
        def _():
            rcopy(far + 1, half).wait_recv()
            dkacc[slot] = dkacc[slot] + rbuf[far, half, 0].astype(F32)
            dvacc[slot] = dvacc[slot] + rbuf[far, half, 1].astype(F32)

    def send_down(far, half):
        sbuf[far - 1, half, 0] = dkacc[half].astype(BF16)
        sbuf[far - 1, half, 1] = dvacc[half].astype(BF16)
        rcopy(far, half).start()

    @pl.when(z >= FAR)
    def _():
        clear(0)
        backward(FAR, 0, 0, HALF, everyone)
        send_down(FAR, 0)

    def backward_step(i, _):
        far, half = (2 * FAR - i) // 2, (i + 1) % 2

        @pl.when(z >= far)
        def _():
            clear(half)
            backward(far, half, 0, ROWS, everyone)

            @pl.when(far < FAR)
            def _():
                add_above(far, half, half)

            send_down(far, half)
        return 0

    lax.fori_loop(0, 2 * FAR - 3, backward_step, 0)

    for slot in range(4):
        clear(slot)
    last = (1, 1, 0, ROWS, 1)
    own = [(0, 0, 0, ROWS, 2), (0, 1, HALF, HALF, 3)]
    pair = GROUP // QUARTERS

    def finish_dq(g, tiles):
        heads = [g * pair + u for u in range(pair)]
        for h, dq in zip(heads, gradients(tiles, heads)):
            dq = (dq * SCALE).astype(BF16)
            for b in range(NX):
                dqbuf[b, :, head(h)] = dq[:, b * TOK:(b + 1) * TOK].T
        xlocal(I_DQ + g).start()
        xsend(I_DQ + g)

    @pl.when(z >= 1)
    def _():
        finish_dq(0, [(1, 0, 0, ROWS, 0), last] + own)
        backward(1, 0, 0, ROWS, everyone[pair:])
        add_above(1, 0, 0)
        send_down(1, 0)

        def step(g, _):
            finish_dq(g, [last] + own)
            return 0
        lax.fori_loop(1, QUARTERS - 1, step, 0)
        backward(1, 1, 0, ROWS, everyone[-pair:])
        add_above(1, 1, 1)
        send_down(1, 1)

    @pl.when(z == 0)
    def _():
        def step(g, _):
            finish_dq(g, own)
            return 0
        lax.fori_loop(0, QUARTERS - 1, step, 0)

    finish_dq(QUARTERS - 1, own)
    for half in range(2):
        add_above(0, half, 2 + half)
        fbuf[0, 2 * half:2 * half + 2] = (dkacc[2 + half] * SCALE).astype(BF16).reshape(2, TOK, HD)
        fbuf[1, 2 * half:2 * half + 2] = dvacc[2 + half].astype(BF16).reshape(2, TOK, HD)
        for item in (I_DK, I_DV):
            @pl.when(x // 2 == half)
            def _():
                xlocal(item).start()
            for d in (1, 3, 2):
                @pl.when(peer(d) // 2 == half)
                def _():
                    xcopy(item, d).start()

    for item in [I_O0, I_O1, I_DK, I_DV] + [I_DQ + g for g in range(QUARTERS)]:
        xrecv(item)
    for item in range(ITEMS):
        xsent(item)
    for far in range(FAR):
        @pl.when((z >= far) & (z < NZ - 1))
        def _():
            for item in range(3):
                zcopy(far, item).wait_send()
    for far in range(1, FAR + 1):
        @pl.when(z >= far)
        def _():
            for half in range(2):
                rcopy(far, half).wait_send()


def hand_over(*refs):
    sources, targets, held, sems = refs[:4], refs[4:8], refs[8:12], refs[12]
    loads = [pltpu.make_async_copy(a, b, sems.at[0, i]) for i, (a, b) in enumerate(zip(sources, held))]
    stores = [pltpu.make_async_copy(a, b, sems.at[1, i]) for i, (a, b) in enumerate(zip(held, targets))]
    for load in loads:
        load.start()
    for load, store in zip(loads, stores):
        load.wait()
        store.start()
    for store in stores:
        store.wait()


def per_device(query, keys, values, out_grad, documents):
    wide, narrow = query.shape, keys.shape
    hbm = pl.BlockSpec(memory_space=pl.ANY)
    vmem = pltpu.VMEM
    dma = pltpu.SemaphoreType.DMA
    results = pl.pallas_call(
        kernel,
        out_shape=(
            jax.ShapeDtypeStruct(wide, BF16),
            jax.ShapeDtypeStruct(wide, BF16),
            jax.ShapeDtypeStruct(narrow, BF16),
            jax.ShapeDtypeStruct(narrow, BF16),
        ),
        in_specs=[hbm, hbm, hbm, hbm, pl.BlockSpec(memory_space=pltpu.VMEM)],
        out_specs=(hbm, hbm, hbm, hbm),
        scratch_shapes=[
            vmem((FAR + 1, NX, TOK, HD), BF16),
            vmem((FAR + 1, NX, TOK, HD), BF16),
            vmem((FAR + 1, NX, 8, TOK), jnp.int32),
            vmem((8, TOK), jnp.int32),
            vmem((FAR + 1, ROWS, HD), BF16),
            vmem((HD, ROWS), BF16),
            vmem((FAR + 1, HD, ROWS), BF16),
            vmem((FAR + 1, HD + PAD, ROWS), BF16),
            vmem((NX, TOK, WIDE), BF16),
            vmem((NX, TOK, WIDE), BF16),
            vmem((GROUP, HD, ROWS), BF16),
            vmem((GROUP, HD, ROWS), BF16),
            vmem((FAR + 1, GROUP, ROWS, ROWS), BF16),
            vmem((GROUP, 1, ROWS), F32),
            vmem((FAR + 1, 2, GROUP, 1, ROWS), F32),
            vmem((GROUP, 1, ROWS), F32),
            vmem((GROUP, 1, ROWS), F32),
            vmem((GROUP, HD + PAD, ROWS), F32),
            vmem((GROUP, HD, ROWS), F32),
            vmem((4, HALF, HD), F32),
            vmem((4, HALF, HD), F32),
            vmem((NX, TOK, WIDE), BF16),
            vmem((NX, TOK, WIDE), BF16),
            vmem((FAR, 2, 2, HALF, HD), BF16),
            vmem((FAR, 2, 2, HALF, HD), BF16),
            vmem((2, NX, TOK, HD), BF16),
            dma((ITEMS, NX)), dma((ITEMS, NX)),
            dma((FAR, 3)), dma((FAR, 3)),
            dma((FAR, 2)), dma((FAR, 2)),
        ],
        compiler_params=pltpu.CompilerParams(
            collective_id=0, has_side_effects=True, vmem_limit_bytes=56 * 2**20
        ),
        cost_estimate=pl.CostEstimate(flops=13 * 10**9, bytes_accessed=9 * 2**20, transcendentals=9 * 10**6),
        name="attention_both_ways",
    )(query, keys, values, out_grad, documents.reshape(1, TOK))
    return pl.pallas_call(
        hand_over,
        out_shape=tuple(jax.ShapeDtypeStruct(r.shape, r.dtype) for r in results),
        in_specs=[hbm] * 4,
        out_specs=(hbm,) * 4,
        scratch_shapes=[vmem(r.shape, r.dtype) for r in results] + [dma((2, 4))],
        compiler_params=pltpu.CompilerParams(vmem_limit_bytes=56 * 2**20),
        cost_estimate=pl.CostEstimate(flops=0, bytes_accessed=5 * 2**20, transcendentals=0),
        name="hand_over",
    )(*results)


def solution(mesh):
    spec = P(("grp", "sp"), None)
    return jax.shard_map(
        per_device,
        mesh=mesh,
        in_specs=(spec, spec, spec, spec, P(("grp", "sp"))),
        out_specs=(spec, spec, spec, spec),
        check_vma=False,
    )
```
